32 devices in a mesh: dp: 8 (over z, y), mp: 4 (over x, core).
Axes of the slice: x: 2, y: 2, z: 4, core: 2. Of those that a mesh axis runs over, the one named last changes fastest.
Arguments:
- hidden: bfloat16 [2048, 8192], P('dp', 'mp'), may hold values from -6 to 6
- target_gain: float32 [8192], replicated, may hold values from 0.1 to 1.9
- target_weight: bfloat16 [2048, 8192], P('mp'), may hold values from -0.0625 to 0.0625
- draft_gain: float32 [8192], P('mp'), may hold values from 0.1 to 1.9
- draft_weight: bfloat16 [2048, 8192], P('dp', 'mp'), may hold values from -0.0625 to 0.0625
- logits: bfloat16 [2048, 32000], P('dp', 'mp'), may hold values from -40 to 300
- seq_lens: int32 [8, 2], P('dp'), may hold values from 32 to 128, as said below
- tool_mask: int32 [2048], P('dp'), may hold values 0 or 1
- owners: int32 [2048, 1], P('dp'), may hold values from 0 to 7; in each aligned block of 256 rows (0 to 255, 256 to 511, ...) at most 40 rows name the same one
Outputs:
- grad_weight: float32 [2048, 8192], P('dp', 'mp')
- grad_gain: float32 [8192], P('mp')
- slot_loss: float32 [2560], P('dp')
The draws below stay inside these ranges and needn't reach their ends.
Inputs may be any that keep to these rules, and one draw needn't show every extreme that they name: `owners`: in the rows of one index of dp at most 40 name the same owner, a bound that some block reaches. `seq_lens`: in each index of dp some sequence has length exactly 128.
All inputs are finite; a program needn't handle non-finite values. No bound on the sum of `tool_mask` on one device may be relied on, other than what follows from the above.
Results may differ from the reference program's by a relative error of at most 0.0085.
Values may be sent and summed in bfloat16 or wider, within the bound.
A program may use at most 128 MiB of HBM per device.

```python
import math
import jax
import jax.numpy as jnp
import numpy as np
from jax import lax

D = 8192
VOCAB = 32000
LEN = 128
SEQS = 2
KVW = 2048
TOK = 256
GROUPS = 8
TOKENS = 2048
CAP = 40
N_DP = 8


def draw_logits(key, part):
    keys = jax.random.split(key, 2)
    spread = jnp.exp(jax.random.uniform(keys[0], (TOKENS, 1), minval=0.0, maxval=math.log(4.0)))
    values = jnp.clip(3.0 * spread * jax.random.normal(keys[1], (TOKENS, VOCAB)), -40.0, 40.0)
    return values.astype(jnp.bfloat16)


def draw_seq_lens(key, part):
    keys = jax.random.split(jax.random.fold_in(key, 17), 2)
    lengths = jax.random.randint(keys[0], (GROUPS, SEQS), LEN // 4, LEN + 1)
    longest = jax.random.randint(keys[1], (GROUPS, 1), 0, SEQS)
    column = jnp.arange(SEQS, dtype=jnp.int32)[None, :]
    return jnp.where(column == longest, LEN, lengths).astype(jnp.int32)


def place_ends(array, key, least, high):
    dims = array.shape
    spot = [jax.random.randint(jax.random.fold_in(key, axis), (), 0, dims[axis]) for axis in range(len(dims))]
    array = array.at[tuple(spot)].set(least)
    longest = dims.index(max(dims))
    spot[longest] = (spot[longest] + 1) % dims[longest]
    return array.at[tuple(spot)].set(high)


def block_levels(own_key, extent, pieces, least, largest):
    def one(dim, parts):
        heights = jax.random.uniform(jax.random.fold_in(jax.random.fold_in(own_key, 6), dim), (parts,), jnp.float32, least / len(pieces), largest / len(pieces))
        return jnp.repeat(jnp.exp(heights), extent[dim] // parts).reshape((-1,) + (1,) * (len(extent) - dim - 1))

    loudness = one(*pieces[0])
    for cut in pieces[1:]:
        loudness = loudness * one(*cut)
    return loudness


def shared_out(rng, own, number, rows, count, top, bound, lean):
    ranking = jax.random.permutation(rng, count)
    crowded, ordinary = load_shares(count, rows * top, bound, lean, True), load_shares(count, rows * top, bound, lean, False)
    places = jnp.arange(count)

    def named(sizes, rotation):
        used = int((sizes > 0).sum())
        fixed = max(1, used // 4)
        moved = fixed + (places - fixed + rotation * (used - fixed)) % max(1, count - fixed)
        return jnp.zeros((count,), jnp.int32).at[ranking[jnp.where(places < fixed, places, moved)]].set(jnp.asarray(sizes, jnp.int32))

    sizes = jnp.where(number % 4 == 0, named(crowded, number // 4), named(ordinary, number - number // 4 - 1))
    mixed = jax.random.permutation(jax.random.fold_in(own, 3), count)
    source_of, sink = mixed[0:count // 2 * 2:2], mixed[1:count // 2 * 2:2]
    slack = jnp.minimum(sizes[source_of] - 1, bound - sizes[sink]) // 2
    slack = jnp.where((source_of == ranking[0]) | (sink == ranking[0]) | (sizes[sink] == 0), 0, jnp.maximum(slack, 0))
    moved = jax.random.randint(jax.random.fold_in(own, 4), (count // 2,), 0, 1 << 20) % (slack + 1)
    sizes = sizes.at[source_of].add(-moved).at[sink].add(moved)
    items = jnp.searchsorted(jnp.cumsum(sizes), jnp.arange(rows * top), side="right").astype(jnp.int32)
    grid = items.reshape(top, rows).T
    grid = grid[jax.random.permutation(jax.random.fold_in(own, 1), rows)]
    rotation = jax.random.randint(jax.random.fold_in(own, 2), (rows, 1), 0, top)
    return jnp.take_along_axis(grid, (jnp.arange(top)[None, :] + rotation) % top, axis=1)


def load_shares(count, total, most, lean, full):
    portions = [(1 << 20) // math.isqrt(standing ** lean) + 1 for standing in range(1, count + 1)]
    largest = most if full else min(most, max(-(-total // count), total * portions[0] // sum(portions)))
    least = 1 if total - largest >= count - 1 else 0
    counts, surplus = [largest] + [least] * (count - 1), total - largest - least * (count - 1)
    while surplus > 0:
        free = [i for i in range(1, count) if counts[i] < largest] or [i for i in range(1, count) if counts[i] < most]
        mass, remaining = sum([portions[i] for i in free]), surplus
        for i in free:
            more = min(most - counts[i], max(1, remaining * portions[i] // mass), surplus)
            counts[i] = counts[i] + more
            surplus = surplus - more
    return np.array(counts)


def centred(rng, shape, scale, limit, cuts=(), kind=jnp.bfloat16):
    array = jax.random.normal(rng, shape, jnp.float32) * scale
    if len(cuts) > 0:
        array = block_levels(rng, shape, cuts, -0.22, 0.18) * array
    return jnp.clip(array, min=-limit, max=limit).astype(kind)


def setup_inputs(seed: int = 0) -> dict:
    streams_of = jax.random.split(jax.random.key(seed), 10)
    hidden = centred(streams_of[0], (TOKENS, D), 1.0, 6.0, ((0, 8), (1, 4)))
    target_gain = jnp.clip(1.0 + 0.18 * jax.random.normal(streams_of[1], (D,), jnp.float32), 0.1, 1.9)
    target_weight = centred(streams_of[2], (KVW, D), D ** -0.5, 0.0625, ((0, 4),))
    draft_gain = jnp.clip(1.0 + 0.18 * jax.random.normal(streams_of[3], (D,), jnp.float32), 0.1, 1.9)
    draft_weight = centred(streams_of[4], (KVW, D), D ** -0.5, 0.0625, ((0, 8), (1, 4)))
    logits = draw_logits(jax.random.fold_in(streams_of[9], 71), 0)
    seq_lens = draw_seq_lens(jax.random.fold_in(streams_of[9], 71), 0)
    tool_mask = place_ends((jax.random.randint(streams_of[7], (TOKENS,), 0, 4) < 3).astype(jnp.int32), jax.random.fold_in(streams_of[7], 1), 0, 1)
    owners_keys = jax.random.split(jax.random.fold_in(streams_of[8], 1), TOKENS // TOK)
    owners_turns = jax.random.permutation(jax.random.fold_in(streams_of[8], 3), TOKENS // TOK)
    owners = jax.vmap(lambda own, number: shared_out(jax.random.fold_in(streams_of[8], 2), own, number, TOK, N_DP, 1, CAP, 2))(owners_keys, owners_turns).reshape((TOKENS, 1))
    return dict(hidden=hidden, target_gain=target_gain, target_weight=target_weight, draft_gain=draft_gain, draft_weight=draft_weight, logits=logits, seq_lens=seq_lens, tool_mask=tool_mask, owners=owners)


EPSILON = 1e-05

def row_entropy(block):
    values = block.astype(jnp.float32)
    highest = lax.optimization_barrier(jnp.max(values, axis=1))
    shifted = values - highest[:, None]
    expsum = jnp.exp(shifted)
    total = lax.optimization_barrier(jnp.sum(expsum, axis=1))
    moment = lax.optimization_barrier(jnp.sum(expsum * shifted, axis=1))
    return jnp.log(total) - moment / total

def reference(hidden, target_gain, target_weight, draft_gain, draft_weight, logits, seq_lens, tool_mask, owners):
    hidden_float = hidden.astype(jnp.float32)
    inverse = lax.rsqrt(lax.optimization_barrier(jnp.mean(hidden_float * hidden_float, axis=1)) + EPSILON)
    target_in = (hidden_float * inverse[:, None] * target_gain).astype(jnp.bfloat16)
    teacher = jnp.dot(target_in, target_weight.T, preferred_element_type=jnp.float32).astype(jnp.bfloat16)
    entropy = lax.map(row_entropy, logits.reshape(N_DP, TOK, VOCAB)).reshape(TOKENS)
    index = jnp.arange(TOKENS, dtype=jnp.int32)
    local_row = index % TOK
    group = index // TOK
    position = local_row % LEN
    sequence = local_row // LEN
    length = seq_lens[group, sequence]
    valid = jnp.logical_and(position < length - 1, tool_mask == 1).astype(jnp.float32)
    weight_low = (valid * entropy / math.log(VOCAB)).astype(jnp.bfloat16)
    weight = lax.optimization_barrier(weight_low).astype(jnp.float32)
    draft_in = (hidden_float * inverse[:, None] * draft_gain).astype(jnp.bfloat16)
    projection = jnp.dot(draft_in, draft_weight.T, preferred_element_type=jnp.float32)
    error = projection - teacher.astype(jnp.float32)
    scale = 1.0 / math.sqrt(TOKENS)
    grad_out = (weight[:, None] * error * scale).astype(jnp.bfloat16)
    row_loss = 0.5 * weight * lax.optimization_barrier(jnp.sum(error * error, axis=1)) * scale
    grad_weight = jnp.dot(grad_out.T, draft_in, preferred_element_type=jnp.float32)
    grad_normed = jnp.dot(grad_out, draft_weight, preferred_element_type=jnp.float32)
    grad_gain = lax.optimization_barrier(jnp.sum(grad_normed * hidden_float * inverse[:, None], axis=0))
    owner = owners[:, 0]
    member = (owner[:, None] == jnp.arange(N_DP, dtype=jnp.int32)[None, :]).astype(jnp.int32)
    member = member.reshape(N_DP, TOK, N_DP)
    running = jnp.cumsum(member, axis=1)
    rank = (lax.optimization_barrier(jnp.sum(running * member, axis=2)) - 1).reshape(TOKENS)
    target_slot = owner * (N_DP * CAP) + group * CAP + rank
    slot_loss = jnp.zeros((N_DP * N_DP * CAP,), jnp.float32).at[target_slot].set(row_loss)
    return (grad_weight, grad_gain, slot_loss)
```

```python
import functools
import math

import jax
import jax.numpy as jnp
from jax import lax
from jax.experimental import pallas as pl
from jax.experimental.pallas import tpu as pltpu
from jax.sharding import PartitionSpec as P

LEN = 128
SEQS = 2
EPSILON = 1e-05
MESH = pl.DeviceIdType.MESH
F32 = jnp.float32
BF16 = jnp.bfloat16


def place_of(index, n):
    odd = lax.rem(index, 2)
    half = lax.div(index, 2)
    return (1 - odd) * half + odd * (n - 1 - half)


def index_of(place, n):
    late = lax.div(place, n // 2)
    return (1 - late) * (2 * place) + late * (2 * (n - 1 - place) + 1)


def kernel(
    n, k,
    hidden, tw, dw, logits, gd, gt, info,
    gw, gain_out, loss_out, msg_out,
    hid, lbuf, twb, wd, sbuf, st, smsg, cmsg, qf, gf,
    local_sem, ring_send, ring_recv, tw_send, tw_recv, ex_send, ex_recv,
    st_send, st_recv, c_send, c_recv, q_send, q_recv, g_send, g_recv,
):
    rows, width = hidden.shape
    kvb = dw.shape[0]
    half = rows // 2
    vocab = logits.shape[1] * k
    d = lax.axis_index("dp")
    m = lax.axis_index("mp")
    place = place_of(d, n)
    right = index_of(lax.rem(place + 1, n), n)
    left = index_of(lax.rem(place + n - 1, n), n)
    holder = lax.div(d * k, n)
    offset = pl.multiple_of(d * kvb - holder * tw.shape[0], 16)

    own_hidden = pltpu.make_async_copy(hidden, hid.at[0], local_sem.at[0])
    own_logits = pltpu.make_async_copy(logits, lbuf, local_sem.at[1])
    own_hidden.start()
    own_logits.start()

    barrier = pltpu.get_barrier_semaphore()
    for j in range(1, n):
        pl.semaphore_signal(
            barrier, inc=1, device_id={"dp": lax.rem(d + j, n)}, device_id_type=MESH
        )
    for j in range(1, k):
        pl.semaphore_signal(
            barrier, inc=1, device_id={"mp": lax.rem(m + j, k)}, device_id_type=MESH
        )
    pl.semaphore_wait(barrier, n - 1 + k - 1)

    def ring(way, t, h, first=False):
        part = pl.ds(h * half, half)
        if way == 0:
            source, target, to = t - 1, t, right
        else:
            source, target, to = lax.rem(n - t + 1, n), n - t, left
        return pltpu.make_async_remote_copy(
            src_ref=hidden.at[part] if first else hid.at[source, part],
            dst_ref=hid.at[target, part],
            send_sem=ring_send.at[way, t, h],
            recv_sem=ring_recv.at[way, t, h],
            device_id={"dp": to},
            device_id_type=MESH,
        )

    for h in (0, 1):
        for way in (0, 1):
            ring(way, 1, h if way == 0 else 1 - h, True).start()

    def tw_columns(index):
        return tw.at[pl.ds(offset, kvb), pl.ds(pl.multiple_of(index * width, width), width)]

    def tw_copy(j):
        to = lax.rem(m + j, k)
        return pltpu.make_async_remote_copy(
            src_ref=tw_columns(to), dst_ref=twb,
            send_sem=tw_send.at[j], recv_sem=tw_recv,
            device_id={"mp": to}, device_id_type=MESH,
        )

    tw_own = pltpu.make_async_copy(tw_columns(m), twb, local_sem.at[2])

    @pl.when(m == holder)
    def _():
        for j in range(1, k):
            tw_copy(j).start()
        tw_own.start()

    own_hidden.wait()
    own_logits.wait()

    def row_stats(i, carry):
        r = pl.ds(pl.multiple_of(i * 16, 16), 16)
        values = lbuf[r, :].astype(F32)
        highest = jnp.max(values, axis=1, keepdims=True)
        shifted = values - highest
        expsum = jnp.exp(shifted)
        total = jnp.sum(expsum, axis=1, keepdims=True)
        moment = jnp.sum(expsum * shifted, axis=1, keepdims=True)
        features = hid[0, r, :].astype(F32)
        squares = jnp.sum(features * features, axis=1, keepdims=True)
        lane = lax.broadcasted_iota(jnp.int32, (16, 128), 1)
        st[r, :] = jnp.where(
            lane == 0, highest, jnp.where(lane == 1, total, jnp.where(lane == 2, moment, squares))
        )
        return carry

    lax.fori_loop(0, rows // 16, row_stats, 0)
    smsg[m] = st[...].T[0:8, :]

    def st_copy(j):
        return pltpu.make_async_remote_copy(
            src_ref=smsg.at[m], dst_ref=smsg.at[m],
            send_sem=st_send.at[j], recv_sem=st_recv.at[j],
            device_id={"mp": lax.rem(m + j, k)}, device_id_type=MESH,
        )

    for j in range(1, k):
        st_copy(j).start()
    for j in range(1, k):
        st_copy(j).wait()
    highest = smsg[0, 0:1, :]
    for j in range(1, k):
        highest = jnp.maximum(highest, smsg[j, 0:1, :])
    total = jnp.zeros_like(highest)
    moment = jnp.zeros_like(highest)
    squares = jnp.zeros_like(highest)
    for j in range(k):
        below = smsg[j, 0:1, :] - highest
        factor = jnp.exp(below)
        total += factor * smsg[j, 1:2, :]
        moment += factor * (smsg[j, 2:3, :] + below * smsg[j, 1:2, :])
        squares += smsg[j, 3:4, :]
    inverse = lax.rsqrt(squares / (width * k) + EPSILON)
    entropy = jnp.log(total) - moment / total
    weight = (info[0:1, :] * entropy / math.log(vocab)).astype(BF16).astype(F32)
    factor = weight * inverse * inverse * (1.0 / math.sqrt(rows * n))
    line = lax.broadcasted_iota(jnp.int32, (8, rows), 0)
    cmsg[d] = jnp.where(line == 0, factor, info[1:2, :])

    def c_copy(j):
        return pltpu.make_async_remote_copy(
            src_ref=cmsg.at[d], dst_ref=cmsg.at[d],
            send_sem=c_send.at[j], recv_sem=c_recv.at[j],
            device_id={"dp": lax.rem(d + j, n)}, device_id_type=MESH,
        )

    for j in range(1, n):
        c_copy(j).start()
    gw[...] = jnp.zeros_like(gw)

    def arrive(t, last, onward):
        for h in (0, 1):
            for way in (0, 1):
                part = h if way == 0 else 1 - h
                if last and h == 1:
                    continue
                ring(way, t, part).wait_recv()
                if h == 0:
                    if onward:
                        ring(way, t + 1, part).start()
                elif onward:
                    @pl.when(t + 1 < n // 2)
                    def _():
                        ring(way, t + 1, part).start()

    arrive(1, n == 2, n > 2)

    @pl.when(m == holder)
    def _():
        tw_own.wait()
        for j in range(1, k):
            tw_copy(j).wait_send()

    @pl.when(m != holder)
    def _():
        tw_copy(1).wait_recv()

    gt_part = gt[:, pl.ds(pl.multiple_of(m * width, width), width)]

    def blend(i, carry):
        r = pl.ds(pl.multiple_of(i * 16, 16), 16)
        wd[r, :] = (
            gd[...] * dw[r, :].astype(F32) - gt_part * twb[r, :].astype(F32)
        ).astype(BF16)
        return carry

    lax.fori_loop(0, kvb // 16, blend, 0)

    def exchange(s, j):
        return pltpu.make_async_remote_copy(
            src_ref=sbuf.at[s, m], dst_ref=sbuf.at[s, m],
            send_sem=ex_send.at[s, j], recv_sem=ex_recv.at[s, j],
            device_id={"mp": lax.rem(m + j, k)}, device_id_type=MESH,
        )

    def project(s):
        sbuf[s, m] = lax.dot_general(
            hid[s], wd[...], (((1,), (1,)), ((), ())), preferred_element_type=F32
        ).astype(BF16)
        for j in range(1, k):
            exchange(s, j).start()

    piece = min(width, 512)

    def consume(s):
        for j in range(1, k):
            exchange(s, j).wait()
        total = sbuf[s, 0].astype(F32)
        for j in range(1, k):
            total += sbuf[s, j].astype(F32)
        block = index_of(lax.rem(place - s + n, n), n)
        factor = jnp.broadcast_to(cmsg[block][0:1, :], (128, rows)).T[:, 0:1]
        grad = (total * factor).astype(BF16)
        squares = lax.dot_general(
            jnp.ones((8, kvb), F32), total * total, (((1,), (1,)), ((), ())),
            precision=lax.Precision.HIGHEST, preferred_element_type=F32,
        )
        qf[d, block] = squares[0:1, :]
        for c in range(0, width, piece):
            gw[:, c:c + piece] += lax.dot_general(
                grad, hid[s, :, c:c + piece], (((0,), (0,)), ((), ())),
                preferred_element_type=F32,
            )

    project(0)
    for j in range(1, n):
        c_copy(j).wait()

    def step(t, carry):
        project(t)
        project(n - t)

        @pl.when(t + 1 < n // 2)
        def _():
            arrive(t + 1, False, True)

        @pl.when(t + 1 == n // 2)
        def _():
            arrive(n // 2, True, False)

        @pl.when(t == 1)
        def _():
            consume(0)

        @pl.when(t > 1)
        def _():
            consume(t - 1)
            consume(n - t + 1)

        return carry

    lax.fori_loop(1, n // 2, step, 0)
    project(n // 2)
    consume(n // 2 - 1)
    consume(n // 2 + 1)
    consume(n // 2)

    gf[d] = jnp.sum(dw[...].astype(F32) * gw[...], axis=0, keepdims=True)

    def q_copy(j):
        return pltpu.make_async_remote_copy(
            src_ref=qf.at[d], dst_ref=qf.at[d],
            send_sem=q_send.at[j], recv_sem=q_recv.at[j],
            device_id={"dp": lax.rem(d + j, n)}, device_id_type=MESH,
        )

    def g_copy(j):
        return pltpu.make_async_remote_copy(
            src_ref=gf.at[d], dst_ref=gf.at[d],
            send_sem=g_send.at[j], recv_sem=g_recv.at[j],
            device_id={"dp": lax.rem(d + j, n)}, device_id_type=MESH,
        )

    for j in range(1, n):
        q_copy(j).start()
        g_copy(j).start()
    msg_out[...] = cmsg[...]

    def sent(t, carry):
        for way in (0, 1):
            ring(way, t, way).wait_send()

            @pl.when(t < n // 2)
            def _():
                ring(way, t, 1 - way).wait_send()

        return carry

    for way in (0, 1):
        for h in (0, 1):
            ring(way, 1, h, True).wait_send()
    lax.fori_loop(2, n // 2 + 1, sent, 0)
    for j in range(1, n):
        q_copy(j).wait()
        g_copy(j).wait()
    gain = gf[0]
    loss = qf[0]
    for j in range(1, n):
        gain += gf[j]
        loss += qf[j]
    gain_out[...] = gain
    for j in range(n):
        loss_out[j] = loss[j] * (0.5 * cmsg[j, 0:1, :])


def on_device(
    hidden, target_gain, target_weight, draft_gain, draft_weight, logits, seq_lens, tool_mask, owners
):
    n = lax.axis_size("dp")
    k = lax.axis_size("mp")
    rows, width = hidden.shape
    kvb = draft_weight.shape[0]
    capacity = max(2, 5 * rows // (4 * n))
    index = jnp.arange(rows, dtype=jnp.int32)
    position = index % LEN
    lookup = (index // LEN)[:, None] == jnp.arange(SEQS, dtype=jnp.int32)[None, :]
    length = jnp.sum(jnp.where(lookup, seq_lens[0][None, :], 0), axis=1)
    valid = jnp.logical_and(position < length - 1, tool_mask == 1).astype(F32)
    info = jnp.stack([valid, owners[:, 0].astype(F32)])
    anywhere = pl.BlockSpec(memory_space=pl.ANY)
    vmem = pl.BlockSpec(memory_space=pltpu.VMEM)
    dma = pltpu.SemaphoreType.DMA
    gw, gain, loss, messages = pl.pallas_call(
        functools.partial(kernel, n, k),
        out_shape=(
            jax.ShapeDtypeStruct((kvb, width), F32),
            jax.ShapeDtypeStruct((1, width), F32),
            jax.ShapeDtypeStruct((n, 1, rows), F32),
            jax.ShapeDtypeStruct((n, 8, rows), F32),
        ),
        in_specs=[anywhere, anywhere, vmem, anywhere, vmem, vmem, vmem],
        out_specs=(vmem, vmem, vmem, vmem),
        scratch_shapes=[
            pltpu.VMEM((n, rows, width), BF16),
            pltpu.VMEM(logits.shape, BF16),
            pltpu.VMEM((kvb, width), BF16),
            pltpu.VMEM((kvb, width), BF16),
            pltpu.VMEM((n, k, rows, kvb), BF16),
            pltpu.VMEM((rows, 128), F32),
            pltpu.VMEM((k, 8, rows), F32),
            pltpu.VMEM((n, 8, rows), F32),
            pltpu.VMEM((n, n, 1, rows), F32),
            pltpu.VMEM((n, 1, width), F32),
            dma((3,)),
            dma((2, n // 2 + 1, 2)),
            dma((2, n // 2 + 1, 2)),
            dma((k,)),
            dma,
            dma((n, k)),
            dma((n, k)),
            dma((k,)),
            dma((k,)),
            dma((n,)),
            dma((n,)),
            dma((n,)),
            dma((n,)),
            dma((n,)),
            dma((n,)),
        ],
        compiler_params=pltpu.CompilerParams(
            collective_id=0, has_side_effects=True, vmem_limit_bytes=58 << 20
        ),
        cost_estimate=pl.CostEstimate(
            flops=4 * n * rows * width * kvb, bytes_accessed=16 << 20, transcendentals=rows * 8000
        ),
    )(
        hidden, target_weight, draft_weight, logits,
        draft_gain.reshape(1, -1), target_gain.reshape(1, -1), info,
    )
    grad_weight = gw * draft_gain[None, :]
    mine = lax.axis_index("dp").astype(F32)
    member = messages[:, 1, :] == mine
    before = (index[:, None] <= index[None, :]).astype(BF16)
    running = jnp.dot(member.astype(BF16), before, preferred_element_type=F32)
    slots = jnp.arange(1, capacity + 1, dtype=jnp.int32).astype(F32)
    chosen = jnp.logical_and(running[:, None, :] == slots[None, :, None], member[:, None, :])
    slot_loss = jnp.sum(jnp.where(chosen, loss, 0.0), axis=2).reshape(n * capacity)
    return (grad_weight, gain.reshape(width), slot_loss)


def solution(mesh):
    in_specs = (
        P("dp", "mp"), P(), P("mp", None), P("mp"), P("dp", "mp"),
        P("dp", "mp"), P("dp", None), P("dp"), P("dp", None),
    )
    out_specs = (P("dp", "mp"), P("mp"), P("dp"))
    return jax.shard_map(
        on_device, mesh=mesh, in_specs=in_specs, out_specs=out_specs, check_vma=False
    )
```

```python
import functools
import math

import jax
import jax.numpy as jnp
from jax import lax
from jax.experimental import pallas as pl
from jax.experimental.pallas import tpu as pltpu
from jax.sharding import PartitionSpec as P

LEN = 128
SEQS = 2
EPSILON = 1e-05
MESH = pl.DeviceIdType.MESH
F32 = jnp.float32
BF16 = jnp.bfloat16


def place_of(index, n):
    odd = lax.rem(index, 2)
    half = lax.div(index, 2)
    return (1 - odd) * half + odd * (n - 1 - half)


def index_of(place, n):
    late = lax.div(place, n // 2)
    return (1 - late) * (2 * place) + late * (2 * (n - 1 - place) + 1)


def kernel(
    n, k, capacity,
    hidden, tw, dweight, logits, gd, gt, info,
    gw, gain_out, slot_out,
    hid, lbuf, twb, dw, wd, sbuf, st, smsg, cmsg, fac, key, qf, gf, totf,
    local_sem, ring_send, ring_recv, tw_send, tw_recv, ex_send, ex_recv,
    st_send, st_recv, c_send, c_recv, q_send, q_recv, g_send, g_recv,
):
    rows, width = hidden.shape
    kvb = dw.shape[0]
    quarter, half = rows // 4, rows // 2
    vocab = logits.shape[0] * k
    d = lax.axis_index("dp")
    m = lax.axis_index("mp")
    place = place_of(d, n)
    right = index_of(lax.rem(place + 1, n), n)
    left = index_of(lax.rem(place + n - 1, n), n)
    holder = lax.div(d * k, n)
    offset = pl.multiple_of(d * kvb - holder * tw.shape[0], 16)

    own_hidden = pltpu.make_async_copy(hidden, hid.at[0], local_sem.at[0])
    own_logits = pltpu.make_async_copy(logits, lbuf, local_sem.at[1])
    own_weight = pltpu.make_async_copy(dweight, dw, local_sem.at[3])

    barrier = pltpu.get_barrier_semaphore()
    for j in range(1, n):
        pl.semaphore_signal(
            barrier, inc=1, device_id={"dp": lax.rem(d + j, n)}, device_id_type=MESH
        )
    for j in range(1, k):
        pl.semaphore_signal(
            barrier, inc=1, device_id={"mp": lax.rem(m + j, k)}, device_id_type=MESH
        )
    own_hidden.start()
    own_logits.start()
    own_weight.start()
    pl.semaphore_wait(barrier, n - 1 + k - 1)

    def ring(way, t, q, first=False):
        part = pl.ds(q * quarter, quarter)
        if way == 0:
            source, target, to = t - 1, t, right
        else:
            source, target, to = lax.rem(n - t + 1, n), n - t, left
        return pltpu.make_async_remote_copy(
            src_ref=hidden.at[part] if first else hid.at[source, part],
            dst_ref=hid.at[target, part],
            send_sem=ring_send.at[way, t, q],
            recv_sem=ring_recv.at[way, t, q],
            device_id={"dp": to},
            device_id_type=MESH,
        )

    def turn(way, i):
        return i if way == 0 else 3 - i

    for i in range(4):
        for way in (0, 1):
            ring(way, 1, turn(way, i), True).start()

    def tw_columns(index):
        return tw.at[pl.ds(offset, kvb), pl.ds(pl.multiple_of(index * width, width), width)]

    def tw_copy(j):
        to = lax.rem(m + j, k)
        return pltpu.make_async_remote_copy(
            src_ref=tw_columns(to), dst_ref=twb,
            send_sem=tw_send.at[j], recv_sem=tw_recv,
            device_id={"mp": to}, device_id_type=MESH,
        )

    tw_own = pltpu.make_async_copy(tw_columns(m), twb, local_sem.at[2])

    @pl.when(m == holder)
    def _():
        for j in range(1, k):
            tw_copy(j).start()
        tw_own.start()

    own_hidden.wait()
    own_logits.wait()
    own_weight.wait()
    entries = logits.shape[0]
    chunk = max(c for c in range(8, 168, 8) if entries % c == 0)

    def folded(values, combine):
        return combine(values.reshape(chunk // 8, 8, rows), axis=0)

    def entries_of(i):
        return lbuf[pl.ds(pl.multiple_of(i * chunk, chunk), chunk), :].astype(F32)

    def largest(i, so_far):
        return jnp.maximum(so_far, folded(entries_of(i), jnp.max))

    highest = lax.fori_loop(
        0, entries // chunk, largest, jnp.full((8, rows), -jnp.inf, F32)
    )
    highest = jnp.max(highest, axis=0, keepdims=True)

    def sums(i, carry):
        shifted = entries_of(i) - highest
        expsum = jnp.exp(shifted)
        return carry[0] + folded(expsum, jnp.sum), carry[1] + folded(expsum * shifted, jnp.sum)

    zero = jnp.zeros((8, rows), F32)
    total, moment = lax.fori_loop(0, entries // chunk, sums, (zero, zero))
    total = jnp.sum(total, axis=0, keepdims=True)
    moment = jnp.sum(moment, axis=0, keepdims=True)

    def row_squares(i, carry):
        r = pl.ds(pl.multiple_of(i * 16, 16), 16)
        features = hid[0, r, :].astype(F32)
        features = features * features
        part = features[:, 0:128]
        for c in range(128, width, 128):
            part += features[:, c:c + 128]
        st[r, :] = part
        return carry

    lax.fori_loop(0, rows // 16, row_squares, 0)
    squares = jnp.sum(st[...].T, axis=0, keepdims=True)
    line = lax.broadcasted_iota(jnp.int32, (8, rows), 0)
    smsg[m] = jnp.where(
        line == 0, highest, jnp.where(line == 1, total, jnp.where(line == 2, moment, squares))
    )

    def st_copy(j):
        return pltpu.make_async_remote_copy(
            src_ref=smsg.at[m], dst_ref=smsg.at[m],
            send_sem=st_send.at[j], recv_sem=st_recv.at[j],
            device_id={"mp": lax.rem(m + j, k)}, device_id_type=MESH,
        )

    for j in range(1, k):
        st_copy(j).start()
    gw[...] = jnp.zeros_like(gw)
    for j in range(1, k):
        st_copy(j).wait()
    highest = smsg[0, 0:1, :]
    for j in range(1, k):
        highest = jnp.maximum(highest, smsg[j, 0:1, :])
    total = jnp.zeros_like(highest)
    moment = jnp.zeros_like(highest)
    squares = jnp.zeros_like(highest)
    for j in range(k):
        below = smsg[j, 0:1, :] - highest
        factor = jnp.exp(below)
        total += factor * smsg[j, 1:2, :]
        moment += factor * (smsg[j, 2:3, :] + below * smsg[j, 1:2, :])
        squares += smsg[j, 3:4, :]
    inverse = lax.rsqrt(squares / (width * k) + EPSILON)
    entropy = jnp.log(total) - moment / total
    weight = (info[0:1, :] * entropy / math.log(vocab)).astype(BF16).astype(F32)
    factor = weight * inverse * inverse * (1.0 / math.sqrt(rows * n))
    cmsg[d] = jnp.where(line == 0, factor, info[1:2, :])

    def c_copy(j):
        return pltpu.make_async_remote_copy(
            src_ref=cmsg.at[d], dst_ref=cmsg.at[d],
            send_sem=c_send.at[j], recv_sem=c_recv.at[j],
            device_id={"dp": lax.rem(d + j, n)}, device_id_type=MESH,
        )

    for j in range(1, n):
        c_copy(j).start()

    def arrive(t, i, onward=True):
        for way in (0, 1):
            ring(way, t, turn(way, i)).wait_recv()
            if onward and i < 2:
                ring(way, t + 1, turn(way, i)).start()
            elif onward:
                @pl.when(t + 1 < n // 2)
                def _():
                    ring(way, t + 1, turn(way, i)).start()

    for i in range(4):
        arrive(1, i)

    for j in range(1, n):
        c_copy(j).wait()

    def columns(s, carry):
        block = index_of(lax.rem(place - s + n, n), n)
        fac[s] = jnp.broadcast_to(cmsg[block][0:1, :], (128, rows)).T
        return carry

    lax.fori_loop(0, n, columns, 0)
    mine = (lax.broadcasted_iota(jnp.int32, (1, rows), 1) * 0 + d).astype(F32)
    before = (
        lax.broadcasted_iota(jnp.int32, (rows, rows), 0)
        <= lax.broadcasted_iota(jnp.int32, (rows, rows), 1)
    ).astype(F32).astype(BF16)

    def slots(j, carry):
        member = jnp.where(cmsg[j] == mine, 1.0, 0.0)
        member = jnp.where(line == 1, member, 0.0)
        running = jnp.dot(member.astype(BF16), before, preferred_element_type=F32)
        key[j] = (running * member)[1:2, :]
        return carry

    lax.fori_loop(0, n, slots, 0)

    @pl.when(m == holder)
    def _():
        tw_own.wait()
        for j in range(1, k):
            tw_copy(j).wait_send()

    @pl.when(m != holder)
    def _():
        tw_copy(1).wait_recv()

    gt_part = gt[:, pl.ds(pl.multiple_of(m * width, width), width)]

    def blend(i, carry):
        r = pl.ds(pl.multiple_of(i * 16, 16), 16)
        wd[r, :] = (
            gd[...] * dw[r, :].astype(F32) - gt_part * twb[r, :].astype(F32)
        ).astype(BF16)
        return carry

    lax.fori_loop(0, kvb // 16, blend, 0)

    def exchange(s, p, start, size, j):
        spot = sbuf.at[s, m, pl.ds(start, size)]
        return pltpu.make_async_remote_copy(
            src_ref=spot, dst_ref=spot,
            send_sem=ex_send.at[s, p, j], recv_sem=ex_recv.at[s, p, j],
            device_id={"mp": lax.rem(m + j, k)}, device_id_type=MESH,
        )

    def project(s, p, start, size):
        sbuf[s, m, start:start + size, :] = lax.dot_general(
            hid[s, start:start + size, :], wd[...], (((1,), (1,)), ((), ())),
            preferred_element_type=F32,
        ).astype(BF16)
        for j in range(1, k):
            exchange(s, p, start, size, j).start()

    piece = min(width, 512)
    ones = jnp.ones((16, kvb), BF16)

    def line_sums(total):
        square = total * total
        high = square.astype(BF16)
        low = (square - high.astype(F32)).astype(BF16)
        over = (((1,), (1,)), ((), ()))
        return (
            lax.dot_general(ones, high, over, preferred_element_type=F32)
            + lax.dot_general(ones, low, over, preferred_element_type=F32)
        )[0:1, :]

    def consume(parts, last=False):
        grads = []
        for s, p, start, size in parts:
            for j in range(1, k):
                exchange(s, p, start, size, j).wait()
            total = sbuf[s, 0, start:start + size, :].astype(F32)
            for j in range(1, k):
                total += sbuf[s, j, start:start + size, :].astype(F32)
            grads.append((total * fac[s, start:start + size, 0:1]).astype(BF16))
            if last:
                totf[start:start + size, :] = total
            else:
                block = index_of(lax.rem(place - s + n, n), n)
                qf[d, block, :, start:start + size] = line_sums(total)
        for c in range(0, width, piece):
            more = gw[:, c:c + piece]
            for (s, p, start, size), grad in zip(parts, grads):
                more += lax.dot_general(
                    grad, hid[s, start:start + size, c:c + piece], (((0,), (0,)), ((), ())),
                    preferred_element_type=F32,
                )
            gw[:, c:c + piece] = more

    def unit(t, u):
        return [(t, u, u * half, half), (n - t, 1 - u, (1 - u) * half, half)]

    def own():
        return [(0, 0, 0, half), (0, 1, half, half)]

    for part in own() + unit(1, 0) + unit(1, 1):
        project(*part)
    consume(own())

    def step(t, carry):
        for u in (0, 1):
            arrive(t, 2 * u)
            arrive(t, 2 * u + 1)
            for part in unit(t, u):
                project(*part)
            consume(unit(t - 1, u))
        return carry

    lax.fori_loop(2, n // 2, step, 0)
    far = n // 2
    outer = [(far, 0, 0, quarter), (far, 1, rows - quarter, quarter)]
    inner = [(far, 2, quarter, half)]
    consume(unit(far - 1, 0))
    arrive(far, 0, False)
    for part in outer:
        project(*part)
    consume(unit(far - 1, 1))
    arrive(far, 1, False)
    for part in inner:
        project(*part)
    consume(outer, True)

    def sent(t, carry):
        for way in (0, 1):
            for i in (0, 1):
                ring(way, t, turn(way, i)).wait_send()

            @pl.when(t < n // 2)
            def _():
                for i in (2, 3):
                    ring(way, t, turn(way, i)).wait_send()

        return carry

    for way in (0, 1):
        for i in range(4):
            ring(way, 1, i, True).wait_send()
    lax.fori_loop(2, n // 2 + 1, sent, 0)
    consume(inner, True)
    qf[d, index_of(lax.rem(place - far + n, n), n)] = line_sums(totf[...])

    def q_copy(j):
        return pltpu.make_async_remote_copy(
            src_ref=qf.at[d], dst_ref=qf.at[d],
            send_sem=q_send.at[j], recv_sem=q_recv.at[j],
            device_id={"dp": lax.rem(d + j, n)}, device_id_type=MESH,
        )

    def g_copy(j):
        return pltpu.make_async_remote_copy(
            src_ref=gf.at[d], dst_ref=gf.at[d],
            send_sem=g_send.at[j], recv_sem=g_recv.at[j],
            device_id={"dp": lax.rem(d + j, n)}, device_id_type=MESH,
        )

    for j in range(1, n):
        q_copy(j).start()
    for c in range(0, width, piece):
        gf[d, :, c:c + piece] = jnp.sum(
            dw[:, c:c + piece].astype(F32) * gw[:, c:c + piece], axis=0, keepdims=True
        )
    for j in range(1, n):
        g_copy(j).start()
    for j in range(1, n):
        q_copy(j).wait()
    loss = qf[0]
    for j in range(1, n):
        loss += qf[j]
    number = (lax.broadcasted_iota(jnp.int32, (capacity, rows), 0) + 1).astype(F32)
    column = lax.broadcasted_iota(jnp.int32, (capacity, 128), 1)
    gathered = jnp.zeros((capacity, 128), F32)
    for j in range(n):
        worth = loss[j] * (0.5 * cmsg[j, 0:1, :])
        held = jnp.sum(jnp.where(number == key[j], worth, 0.0), axis=1, keepdims=True)
        gathered = jnp.where(column == j, held, gathered)
    slot_out[...] = jnp.concatenate(
        [gathered, jnp.zeros((128 - capacity, 128), F32)], axis=0
    ).T[0:n, :]
    for j in range(1, n):
        g_copy(j).wait()
    gain = gf[0]
    for j in range(1, n):
        gain += gf[j]
    gain_out[...] = gain


def on_device(
    hidden, target_gain, target_weight, draft_gain, draft_weight, logits, seq_lens, tool_mask, owners
):
    n = lax.axis_size("dp")
    k = lax.axis_size("mp")
    rows, width = hidden.shape
    kvb = draft_weight.shape[0]
    capacity = max(2, 5 * rows // (4 * n))
    whole_tiles = -(-capacity // 8) * 8
    index = jnp.arange(rows, dtype=jnp.int32)
    position = index % LEN
    lookup = (index // LEN)[:, None] == jnp.arange(SEQS, dtype=jnp.int32)[None, :]
    length = jnp.sum(jnp.where(lookup, seq_lens[0][None, :], 0), axis=1)
    valid = jnp.logical_and(position < length - 1, tool_mask == 1).astype(F32)
    info = jnp.stack([valid, owners[:, 0].astype(F32)])
    anywhere = pl.BlockSpec(memory_space=pl.ANY)
    vmem = pl.BlockSpec(memory_space=pltpu.VMEM)
    dma = pltpu.SemaphoreType.DMA
    gw, gain, slots = pl.pallas_call(
        functools.partial(kernel, n, k, whole_tiles),
        out_shape=(
            jax.ShapeDtypeStruct((kvb, width), F32),
            jax.ShapeDtypeStruct((1, width), F32),
            jax.ShapeDtypeStruct((n, 128), F32),
        ),
        in_specs=[anywhere, anywhere, anywhere, anywhere, vmem, vmem, vmem],
        out_specs=(vmem, vmem, vmem),
        scratch_shapes=[
            pltpu.VMEM((n, rows, width), BF16),
            pltpu.VMEM((logits.shape[1], rows), BF16),
            pltpu.VMEM((kvb, width), BF16),
            pltpu.VMEM((kvb, width), BF16),
            pltpu.VMEM((kvb, width), BF16),
            pltpu.VMEM((n, k, rows, kvb), BF16),
            pltpu.VMEM((rows, 128), F32),
            pltpu.VMEM((k, 8, rows), F32),
            pltpu.VMEM((n, 8, rows), F32),
            pltpu.VMEM((n, rows, 128), F32),
            pltpu.VMEM((n, 1, rows), F32),
            pltpu.VMEM((n, n, 1, rows), F32),
            pltpu.VMEM((n, 1, width), F32),
            pltpu.VMEM((rows, kvb), F32),
            dma((4,)),
            dma((2, n // 2 + 1, 4)),
            dma((2, n // 2 + 1, 4)),
            dma((k,)),
            dma,
            dma((n, 3, k)),
            dma((n, 3, k)),
            dma((k,)),
            dma((k,)),
            dma((n,)),
            dma((n,)),
            dma((n,)),
            dma((n,)),
            dma((n,)),
            dma((n,)),
        ],
        compiler_params=pltpu.CompilerParams(
            collective_id=0, has_side_effects=True, vmem_limit_bytes=58 << 20
        ),
        cost_estimate=pl.CostEstimate(
            flops=4 * n * rows * width * kvb,
            bytes_accessed=2 * (logits.size + 4 * kvb * width),
            transcendentals=logits.size,
        ),
    )(
        hidden, target_weight, draft_weight, logits.T,
        draft_gain.reshape(1, -1), target_gain.reshape(1, -1), info,
    )
    grad_weight = gw * draft_gain[None, :]
    return (grad_weight, gain.reshape(width), slots[:, 0:capacity].reshape(n * capacity))


def solution(mesh):
    in_specs = (
        P("dp", "mp"), P(), P("mp", None), P("mp"), P("dp", "mp"),
        P("dp", "mp"), P("dp", None), P("dp"), P("dp", None),
    )
    out_specs = (P("dp", "mp"), P("mp"), P("dp"))
    return jax.shard_map(
        on_device, mesh=mesh, in_specs=in_specs, out_specs=out_specs, check_vma=False
    )
```

```python
import functools
import math

import jax
import jax.numpy as jnp
from jax import lax
from jax.experimental import pallas as pl
from jax.experimental.pallas import tpu as pltpu
from jax.sharding import PartitionSpec as P

LEN = 128
SEQS = 2
EPSILON = 1e-05
MESH = pl.DeviceIdType.MESH
F32 = jnp.float32
BF16 = jnp.bfloat16


def place_of(index, n):
    odd = lax.rem(index, 2)
    half = lax.div(index, 2)
    return (1 - odd) * half + odd * (n - 1 - half)


def index_of(place, n):
    late = lax.div(place, n // 2)
    return (1 - late) * (2 * place) + late * (2 * (n - 1 - place) + 1)


def kernel(
    n, k, capacity,
    hidden, tw, dweight, logits, gd, gt, lens, mask, owner,
    gw_out, gain_out, slot_out,
    hid, lbuf, twb, dw, wd, sbuf, st, smsg, cmsg, fac, key, qf, gf, totf, gw,
    local_sem, ring_send, ring_recv, tw_send, tw_recv, ex_send, ex_recv,
    st_send, st_recv, c_send, c_recv, q_send, q_recv, g_send, g_recv, out_sem,
):
    rows, width = hidden.shape
    kvb = dw.shape[0]
    quarter, half = rows // 4, rows // 2
    vocab = logits.shape[0] * k
    d = lax.axis_index("dp")
    m = lax.axis_index("mp")
    place = place_of(d, n)
    right = index_of(lax.rem(place + 1, n), n)
    left = index_of(lax.rem(place + n - 1, n), n)
    holder = lax.div(d * k, n)
    offset = pl.multiple_of(d * kvb - holder * tw.shape[0], 16)

    own_hidden = pltpu.make_async_copy(hidden, hid.at[0], local_sem.at[0])
    own_logits = pltpu.make_async_copy(logits, lbuf, local_sem.at[1])
    own_weight = pltpu.make_async_copy(dweight, dw, local_sem.at[3])

    barrier = pltpu.get_barrier_semaphore()
    for j in range(1, n):
        pl.semaphore_signal(
            barrier, inc=1, device_id={"dp": lax.rem(d + j, n)}, device_id_type=MESH
        )
    for j in range(1, k):
        pl.semaphore_signal(
            barrier, inc=1, device_id={"mp": lax.rem(m + j, k)}, device_id_type=MESH
        )
    own_hidden.start()
    own_logits.start()
    own_weight.start()
    pl.semaphore_wait(barrier, n - 1 + k - 1)

    def ring(way, t, q, first=False):
        part = pl.ds(q * quarter, quarter)
        if way == 0:
            source, target, to = t - 1, t, right
        else:
            source, target, to = lax.rem(n - t + 1, n), n - t, left
        return pltpu.make_async_remote_copy(
            src_ref=hidden.at[part] if first else hid.at[source, part],
            dst_ref=hid.at[target, part],
            send_sem=ring_send.at[way, t, q],
            recv_sem=ring_recv.at[way, t, q],
            device_id={"dp": to},
            device_id_type=MESH,
        )

    def turn(way, i):
        return i if way == 0 else 3 - i

    for i in range(4):
        for way in (0, 1):
            ring(way, 1, turn(way, i), True).start()

    def tw_columns(index):
        return tw.at[pl.ds(offset, kvb), pl.ds(pl.multiple_of(index * width, width), width)]

    def tw_copy(j):
        to = lax.rem(m + j, k)
        return pltpu.make_async_remote_copy(
            src_ref=tw_columns(to), dst_ref=twb,
            send_sem=tw_send.at[j], recv_sem=tw_recv,
            device_id={"mp": to}, device_id_type=MESH,
        )

    tw_own = pltpu.make_async_copy(tw_columns(m), twb, local_sem.at[2])

    @pl.when(m == holder)
    def _():
        for j in range(1, k):
            tw_copy(j).start()
        tw_own.start()

    own_hidden.wait()
    own_logits.wait()
    own_weight.wait()
    entries = logits.shape[0]
    chunk = max(c for c in range(8, 168, 8) if entries % c == 0)

    def folded(values, combine):
        return combine(values.reshape(chunk // 8, 8, rows), axis=0)

    def entries_of(i):
        return lbuf[pl.ds(pl.multiple_of(i * chunk, chunk), chunk), :].astype(F32)

    def largest(i, so_far):
        return jnp.maximum(so_far, folded(entries_of(i), jnp.max))

    highest = lax.fori_loop(
        0, entries // chunk, largest, jnp.full((8, rows), -jnp.inf, F32)
    )
    highest = jnp.max(highest, axis=0, keepdims=True)

    def sums(i, carry):
        shifted = entries_of(i) - highest
        expsum = jnp.exp(shifted)
        return carry[0] + folded(expsum, jnp.sum), carry[1] + folded(expsum * shifted, jnp.sum)

    zero = jnp.zeros((8, rows), F32)
    total, moment = lax.fori_loop(0, entries // chunk, sums, (zero, zero))
    total = jnp.sum(total, axis=0, keepdims=True)
    moment = jnp.sum(moment, axis=0, keepdims=True)

    def row_squares(i, carry):
        r = pl.ds(pl.multiple_of(i * 16, 16), 16)
        features = hid[0, r, :].astype(F32)
        features = features * features
        part = features[:, 0:128]
        for c in range(128, width, 128):
            part += features[:, c:c + 128]
        st[r, :] = part
        return carry

    lax.fori_loop(0, rows // 16, row_squares, 0)
    squares = jnp.sum(st[...].T, axis=0, keepdims=True)
    line = lax.broadcasted_iota(jnp.int32, (8, rows), 0)
    smsg[m] = jnp.where(
        line == 0, highest, jnp.where(line == 1, total, jnp.where(line == 2, moment, squares))
    )

    def st_copy(j):
        return pltpu.make_async_remote_copy(
            src_ref=smsg.at[m], dst_ref=smsg.at[m],
            send_sem=st_send.at[j], recv_sem=st_recv.at[j],
            device_id={"mp": lax.rem(m + j, k)}, device_id_type=MESH,
        )

    for j in range(1, k):
        st_copy(j).start()
    gw[...] = jnp.zeros_like(gw)
    qf[d] = jnp.zeros((n, 1, rows), F32)
    for j in range(1, k):
        st_copy(j).wait()
    highest = smsg[0, 0:1, :]
    for j in range(1, k):
        highest = jnp.maximum(highest, smsg[j, 0:1, :])
    total = jnp.zeros_like(highest)
    moment = jnp.zeros_like(highest)
    squares = jnp.zeros_like(highest)
    for j in range(k):
        below = smsg[j, 0:1, :] - highest
        factor = jnp.exp(below)
        total += factor * smsg[j, 1:2, :]
        moment += factor * (smsg[j, 2:3, :] + below * smsg[j, 1:2, :])
        squares += smsg[j, 3:4, :]
    inverse = lax.rsqrt(squares / (width * k) + EPSILON)
    entropy = jnp.log(total) - moment / total
    index = lax.broadcasted_iota(jnp.int32, (1, rows), 1)
    length = jnp.zeros((1, rows), jnp.int32)
    for q in range(rows // LEN):
        length = jnp.where(index // LEN == q, lens[0:1, q:q + 1], length)
    valid = jnp.where(
        jnp.logical_and(index % LEN < length - 1, mask[...] == 1), 1.0, 0.0
    )
    weight = (valid * entropy / math.log(vocab)).astype(BF16).astype(F32)
    factor = weight * inverse * inverse * (1.0 / math.sqrt(rows * n))
    cmsg[d] = jnp.where(line == 0, factor, owner[...].astype(F32))

    def c_copy(j):
        return pltpu.make_async_remote_copy(
            src_ref=cmsg.at[d], dst_ref=cmsg.at[d],
            send_sem=c_send.at[j], recv_sem=c_recv.at[j],
            device_id={"dp": lax.rem(d + j, n)}, device_id_type=MESH,
        )

    for j in range(1, n):
        c_copy(j).start()

    def arrive(t, i, onward=True):
        for way in (0, 1):
            ring(way, t, turn(way, i)).wait_recv()
            if onward and i < 2:
                ring(way, t + 1, turn(way, i)).start()
            elif onward:
                @pl.when(t + 1 < n // 2)
                def _():
                    ring(way, t + 1, turn(way, i)).start()

    for i in range(4):
        arrive(1, i)

    for j in range(1, n):
        c_copy(j).wait()

    def columns(s, carry):
        block = index_of(lax.rem(place - s + n, n), n)
        fac[s] = jnp.broadcast_to(cmsg[block][0:1, :], (128, rows)).T
        return carry

    lax.fori_loop(0, n, columns, 0)
    mine = (lax.broadcasted_iota(jnp.int32, (1, rows), 1) * 0 + d).astype(F32)
    before = (
        lax.broadcasted_iota(jnp.int32, (rows, rows), 0)
        <= lax.broadcasted_iota(jnp.int32, (rows, rows), 1)
    ).astype(F32).astype(BF16)

    def slots(j, carry):
        member = jnp.where(cmsg[j] == mine, 1.0, 0.0)
        member = jnp.where(line == 1, member, 0.0)
        running = jnp.dot(member.astype(BF16), before, preferred_element_type=F32)
        key[j] = (running * member)[1:2, :]
        return carry

    lax.fori_loop(0, n, slots, 0)

    @pl.when(m == holder)
    def _():
        tw_own.wait()
        for j in range(1, k):
            tw_copy(j).wait_send()

    @pl.when(m != holder)
    def _():
        tw_copy(1).wait_recv()

    gt_part = gt[:, pl.ds(pl.multiple_of(m * width, width), width)]

    def blend(i, carry):
        r = pl.ds(pl.multiple_of(i * 16, 16), 16)
        wd[r, :] = (
            gd[...] * dw[r, :].astype(F32) - gt_part * twb[r, :].astype(F32)
        ).astype(BF16)
        return carry

    lax.fori_loop(0, kvb // 16, blend, 0)

    def exchange(s, p, start, size, j):
        spot = sbuf.at[s, m, pl.ds(start, size)]
        return pltpu.make_async_remote_copy(
            src_ref=spot, dst_ref=spot,
            send_sem=ex_send.at[s, p, j], recv_sem=ex_recv.at[s, p, j],
            device_id={"mp": lax.rem(m + j, k)}, device_id_type=MESH,
        )

    def project(s, p, start, size):
        sbuf[s, m, start:start + size, :] = lax.dot_general(
            hid[s, start:start + size, :], wd[...], (((1,), (1,)), ((), ())),
            preferred_element_type=F32,
        ).astype(BF16)
        for j in range(1, k):
            exchange(s, p, start, size, j).start()

    piece = min(width, 512)
    ones = jnp.ones((16, kvb), BF16)

    def line_sums(total):
        square = total * total
        high = square.astype(BF16)
        low = (square - high.astype(F32)).astype(BF16)
        over = (((1,), (1,)), ((), ()))
        return (
            lax.dot_general(ones, high, over, preferred_element_type=F32)
            + lax.dot_general(ones, low, over, preferred_element_type=F32)
        )[0:1, :]

    def write_out(c):
        columns_of = pl.ds(c, piece)
        return pltpu.make_async_copy(
            gw.at[:, columns_of], gw_out.at[:, columns_of], out_sem.at[c // piece]
        )

    def consume(parts, last=False, final=False):
        grads = []
        for s, p, start, size in parts:
            for j in range(1, k):
                exchange(s, p, start, size, j).wait()
            total = sbuf[s, 0, start:start + size, :].astype(F32)
            for j in range(1, k):
                total += sbuf[s, j, start:start + size, :].astype(F32)
            grads.append((total * fac[s, start:start + size, 0:1]).astype(BF16))
            if last:
                totf[start:start + size, :] = total
            else:
                block = index_of(lax.rem(place - s + n, n), n)
                qf[d, block, :, start:start + size] = line_sums(total)
        for c in range(0, width, piece):
            more = gw[:, c:c + piece]
            for (s, p, start, size), grad in zip(parts, grads):
                more += lax.dot_general(
                    grad, hid[s, start:start + size, c:c + piece], (((0,), (0,)), ((), ())),
                    preferred_element_type=F32,
                )
            gw[:, c:c + piece] = more
            if final:
                write_out(c).start()
                gf[d, :, c:c + piece] = jnp.sum(
                    dw[:, c:c + piece].astype(F32) * more, axis=0, keepdims=True
                )

    def unit(t, u):
        return [(t, u, u * half, half), (n - t, 1 - u, (1 - u) * half, half)]

    def own():
        return [(0, 0, 0, half), (0, 1, half, half)]

    for part in own() + unit(1, 0) + unit(1, 1):
        project(*part)
    consume(own())

    def step(t, carry):
        for u in (0, 1):
            arrive(t, 2 * u)
            arrive(t, 2 * u + 1)
            for part in unit(t, u):
                project(*part)
            consume(unit(t - 1, u))
        return carry

    lax.fori_loop(2, n // 2, step, 0)
    far = n // 2
    outer = [(far, 0, 0, quarter), (far, 1, rows - quarter, quarter)]
    inner = [(far, 2, quarter, half)]
    consume(unit(far - 1, 0))
    arrive(far, 0, False)
    for part in outer:
        project(*part)
    consume(unit(far - 1, 1))
    arrive(far, 1, False)
    for part in inner:
        project(*part)

    def q_copy(j):
        return pltpu.make_async_remote_copy(
            src_ref=qf.at[d], dst_ref=qf.at[d],
            send_sem=q_send.at[j], recv_sem=q_recv.at[j],
            device_id={"dp": lax.rem(d + j, n)}, device_id_type=MESH,
        )

    for j in range(1, n):
        q_copy(j).start()
    consume(outer, True)

    def sent(t, carry):
        for way in (0, 1):
            for i in (0, 1):
                ring(way, t, turn(way, i)).wait_send()

            @pl.when(t < n // 2)
            def _():
                for i in (2, 3):
                    ring(way, t, turn(way, i)).wait_send()

        return carry

    for way in (0, 1):
        for i in range(4):
            ring(way, 1, i, True).wait_send()
    lax.fori_loop(2, n // 2 + 1, sent, 0)
    consume(inner, True, True)
    gf[d, :, width:width + rows] = line_sums(totf[...])

    def g_copy(j):
        return pltpu.make_async_remote_copy(
            src_ref=gf.at[d], dst_ref=gf.at[d],
            send_sem=g_send.at[j], recv_sem=g_recv.at[j],
            device_id={"dp": lax.rem(d + j, n)}, device_id_type=MESH,
        )

    for j in range(1, n):
        g_copy(j).start()
    for j in range(1, n):
        q_copy(j).wait()
        g_copy(j).wait()
    gain = gf[0, :, 0:width]
    for j in range(1, n):
        gain += gf[j, :, 0:width]
    gain_out[...] = gain

    def far_of(j):
        spot = (j // 2 if j % 2 == 0 else n - 1 - j // 2) - n // 2
        spot = (spot + n) % n
        return 2 * spot if spot < n // 2 else 2 * (n - 1 - spot) + 1

    loss = []
    for b in range(n):
        lot = jnp.zeros((1, rows), F32)
        for j in range(n):
            lot += gf[j, :, width:width + rows] if far_of(j) == b else qf[j, b]
        loss.append(lot)
    number = (lax.broadcasted_iota(jnp.int32, (capacity, rows), 0) + 1).astype(F32)
    column = lax.broadcasted_iota(jnp.int32, (capacity, 128), 1)
    gathered = jnp.zeros((capacity, 128), F32)
    for j in range(n):
        worth = loss[j] * (0.5 * cmsg[j, 0:1, :])
        held = jnp.sum(jnp.where(number == key[j], worth, 0.0), axis=1, keepdims=True)
        gathered = jnp.where(column == j, held, gathered)
    slot_out[...] = jnp.concatenate(
        [gathered, jnp.zeros((128 - capacity, 128), F32)], axis=0
    ).T[0:n, :]
    for c in range(0, width, piece):
        write_out(c).wait()


def on_device(
    hidden, target_gain, target_weight, draft_gain, draft_weight, logits, seq_lens, tool_mask, owners
):
    n = lax.axis_size("dp")
    k = lax.axis_size("mp")
    rows, width = hidden.shape
    kvb = draft_weight.shape[0]
    capacity = max(2, 5 * rows // (4 * n))
    whole_tiles = -(-capacity // 8) * 8
    lanes = -(-kvb // 128) * 128
    room = 2 * (n * rows * width + logits.size + 3 * kvb * width + n * k * rows * lanes)
    room += 4 * (n * rows * 128 + kvb * width + rows * lanes) + (6 << 20)
    anywhere = pl.BlockSpec(memory_space=pl.ANY)
    vmem = pl.BlockSpec(memory_space=pltpu.VMEM)
    dma = pltpu.SemaphoreType.DMA
    gw, gain, slots = pl.pallas_call(
        functools.partial(kernel, n, k, whole_tiles),
        out_shape=(
            jax.ShapeDtypeStruct((kvb, width), F32),
            jax.ShapeDtypeStruct((1, width), F32),
            jax.ShapeDtypeStruct((n, 128), F32),
        ),
        in_specs=[anywhere] * 4 + [vmem] * 5,
        out_specs=(anywhere, vmem, vmem),
        scratch_shapes=[
            pltpu.VMEM((n, rows, width), BF16),
            pltpu.VMEM((logits.shape[1], rows), BF16),
            pltpu.VMEM((kvb, width), BF16),
            pltpu.VMEM((kvb, width), BF16),
            pltpu.VMEM((kvb, width), BF16),
            pltpu.VMEM((n, k, rows, kvb), BF16),
            pltpu.VMEM((rows, 128), F32),
            pltpu.VMEM((k, 8, rows), F32),
            pltpu.VMEM((n, 8, rows), F32),
            pltpu.VMEM((n, rows, 128), F32),
            pltpu.VMEM((n, 1, rows), F32),
            pltpu.VMEM((n, n, 1, rows), F32),
            pltpu.VMEM((n, 1, width + rows), F32),
            pltpu.VMEM((rows, kvb), F32),
            pltpu.VMEM((kvb, width), F32),
            dma((4,)),
            dma((2, n // 2 + 1, 4)),
            dma((2, n // 2 + 1, 4)),
            dma((k,)),
            dma,
            dma((n, 3, k)),
            dma((n, 3, k)),
            dma((k,)),
            dma((k,)),
            dma((n,)),
            dma((n,)),
            dma((n,)),
            dma((n,)),
            dma((n,)),
            dma((n,)),
            dma((-(-width // 512),)),
        ],
        compiler_params=pltpu.CompilerParams(
            collective_id=0, has_side_effects=True, vmem_limit_bytes=max(room, 58 << 20)
        ),
        cost_estimate=pl.CostEstimate(
            flops=4 * n * rows * width * kvb,
            bytes_accessed=2 * (logits.size + 4 * kvb * width),
            transcendentals=logits.size,
        ),
    )(
        hidden, target_weight, draft_weight, logits.T,
        draft_gain.reshape(1, -1), target_gain.reshape(1, -1),
        seq_lens, tool_mask.reshape(1, -1), owners.T,
    )
    grad_weight = gw * draft_gain[None, :]
    return (grad_weight, gain.reshape(width), slots[:, 0:capacity].reshape(n * capacity))


def solution(mesh):
    in_specs = (
        P("dp", "mp"), P(), P("mp", None), P("mp"), P("dp", "mp"),
        P("dp", "mp"), P("dp", None), P("dp"), P("dp", None),
    )
    out_specs = (P("dp", "mp"), P("mp"), P("dp"))
    return jax.shard_map(
        on_device, mesh=mesh, in_specs=in_specs, out_specs=out_specs, check_vma=False
    )
```
